512 devices in a mesh: tm: 32 (over y, x), dom: 16 (over z, core).
Axes of the slice: x: 4, y: 8, z: 8, core: 2. Of those that a mesh axis runs over, the one named last changes fastest.
Arguments:
- node_pos: float32 [32, 3, 3, 8192], P('tm', None, None, 'dom'), may hold values from -2 to 19
- vorticity: float32 [3, 8192], P(None, 'dom'), may hold values from -0.024414062 to 0.024414062
- coarse_of: int32 [8192], P('dom'), may hold values from 0 to 4095, as said below
Outputs:
- fine_nodes: float32 [32, 3, 3, 8192], P('tm', None, None, 'dom')
- coarse_end: float32 [32, 3, 4096], P('tm', None, 'dom')
The draws below stay inside these ranges and needn't reach their ends.
Inputs may be any that keep to these rules, and one draw needn't show every extreme that they name: coarse_of[i] = (i // 2 + j) mod 4096 for some integer j with -2048 <= j <= 2048; j = 0 for even i; j = 2048 for i = 1 and j = -2048 for i = 3.
All inputs are finite; a program needn't handle non-finite values.
Results may differ from the reference program's by a relative error of at most 0.0003.
Values sent between devices are 32-bit elements; how exact they have to be, the bound alone decides.
No kernel may reach another device: no remote copies, remote signals or barrier semaphores. Data moves between devices by JAX's collectives and lax.ppermute only.
A program may use at most 64 MiB of HBM per device.

```python
import math
import jax
import jax.numpy as jnp
from jax import lax

PARTICLES = 8192
COARSE = 4096
SLICES = 32


def cycle_angles():
    index = jnp.arange(PARTICLES).astype(jnp.float32)
    return 2.0 * math.pi * (index + 0.5) / PARTICLES


def draw_node_pos(key, part):
    angles = cycle_angles()
    core_key = jax.random.fold_in(key, 11)
    first_key, second_key = jax.random.split(core_key)
    radial = 0.25 * jnp.sqrt(jax.random.uniform(first_key, (PARTICLES,), jnp.float32))
    beside_all = 2.0 * math.pi * jax.random.uniform(second_key, (PARTICLES,), jnp.float32)
    spread = 1.0 + radial * jnp.cos(beside_all)
    base = jnp.stack([spread * jnp.cos(angles), spread * jnp.sin(angles), radial * jnp.sin(beside_all)], 0)
    times = (jnp.arange(SLICES).astype(jnp.float32)[:, None] + jnp.array([0.0, 0.5, 1.0], jnp.float32)[None, :]) * 0.5
    lifted = times[:, :, None, None] * jnp.array([0.0, 0.0, 1.0], jnp.float32)[None, None, :, None]
    noise_key = jax.random.fold_in(key, 23)
    noise = 0.05 * jax.random.normal(noise_key, (SLICES, 3, 3, PARTICLES), jnp.float32)
    return base[None, None] + lifted + noise


def draw_vorticity(key, part):
    angles = cycle_angles()
    first_key, second_key = jax.random.split(jax.random.fold_in(key, 37))
    strength = jnp.exp(jax.random.uniform(first_key, (PARTICLES,), jnp.float32, math.log(0.5), math.log(2.0)))
    scale = 4.0 * 2.0 * math.pi / PARTICLES * strength
    tangent = jnp.stack([-jnp.sin(angles), jnp.cos(angles), jnp.zeros_like(angles)], 0)
    noise = jnp.clip(jax.random.normal(second_key, (3, PARTICLES), jnp.float32), -3.0, 3.0)
    return scale[None, :] * (tangent + 0.3 * noise)


def draw_coarse_of(key, part):
    index = jnp.arange(PARTICLES, dtype=jnp.int32)
    half_reach = COARSE // 2
    jitter = jax.random.randint(jax.random.fold_in(key, 53), (PARTICLES,), -half_reach, half_reach + 1, jnp.int32)
    jitter = jnp.where(index % 2 == 0, 0, jitter)
    jitter = jnp.where(index == 1, half_reach, jnp.where(index == 3, -half_reach, jitter))
    return jnp.mod(index // 2 + jitter, COARSE).astype(jnp.int32)


def setup_inputs(seed: int = 0) -> dict:
    splits = jax.random.split(jax.random.key(seed), 4)
    node_pos = draw_node_pos(jax.random.fold_in(splits[3], 71), 0)
    vorticity = draw_vorticity(jax.random.fold_in(splits[3], 71), 0)
    coarse_of = draw_coarse_of(jax.random.fold_in(splits[3], 71), 0)
    return {"node_pos": node_pos, "vorticity": vorticity, "coarse_of": coarse_of}


inv_four_pi = 1.0 / (4.0 * math.pi)
sigma_sq = 0.01
dt_slice = 0.5
node_weights = ((5.0 / 24.0, 1.0 / 3.0, -1.0 / 24.0), (-1.0 / 24.0, 1.0 / 3.0, 5.0 / 24.0))

def pair_field(targets, sources, strengths):
    offsets = targets[:, :, None] - sources[:, None, :]
    radius_sq = lax.optimization_barrier(jnp.sum(offsets * offsets, axis=0)) + sigma_sq
    kernel = inv_four_pi / (radius_sq * jnp.sqrt(radius_sq))
    moments = jnp.concatenate([strengths, jnp.cross(strengths, sources, axis=0)], 0)
    summed = jnp.einsum('ts,cs->ct', kernel, moments, precision=lax.Precision.HIGHEST)
    return jnp.cross(summed[:3], targets, axis=0) - summed[3:]

def velocity_of(positions, vorticity):
    total = positions.shape[1]
    width = math.gcd(total, 512)
    blocks = positions.reshape(3, total // width, width).transpose(1, 0, 2)
    result = lax.map(lambda block: pair_field(block, positions, vorticity), blocks)
    return result.transpose(1, 0, 2).reshape(3, total)

def sweep_slice(states, vorticity):
    velocity = [velocity_of(states[node_index], vorticity) for node_index in range(3)]
    quad_old = [dt_slice * (row[0] * velocity[0] + row[1] * velocity[1] + row[2] * velocity[2]) for row in node_weights]
    first = states[0]
    second = first + quad_old[0]
    swept_two = velocity_of(second, vorticity)
    third = second + 0.5 * dt_slice * (swept_two - velocity[1]) + quad_old[1]
    swept_three = velocity_of(third, vorticity)
    quad_new = [dt_slice * (row[0] * velocity[0] + row[1] * swept_two + row[2] * swept_three) for row in node_weights]
    return jnp.concatenate([first, second, third, quad_new[0], quad_new[1]], 0)

def reference(node_pos, vorticity, coarse_of):
    rows = lax.map(lambda states: sweep_slice(states, vorticity), node_pos)
    sums = jax.vmap(lambda block: jax.ops.segment_sum(block.T, coarse_of, COARSE).T)(rows)
    counts = jax.ops.segment_sum(jnp.ones((PARTICLES,), jnp.float32), coarse_of, COARSE)
    means = sums / counts
    built = means[:, :9].reshape(SLICES, 3, 3, COARSE)
    early = means[:, 9:12]
    late = means[:, 12:15]
    advance = early + late
    running = jnp.cumsum(advance, 0)
    begin = jnp.concatenate([built[0:1, 0], built[0, 0][None] + running[:-1]], 0)
    ends = jnp.stack([begin, begin + early, begin + advance], 1)
    correction = ends - built
    fine_nodes = rows[:, :9].reshape(SLICES, 3, 3, PARTICLES) + correction[:, :, :, coarse_of]
    return (fine_nodes, begin + advance)
```

```python
import math

import jax
import jax.numpy as jnp
from jax import lax
from jax.experimental import pallas as pl
from jax.experimental.pallas import tpu as pltpu
from jax.sharding import PartitionSpec as P

f32 = jnp.float32
bf16 = jnp.bfloat16
inv_four_pi = 1.0 / (4.0 * math.pi)
sigma_sq = 0.01
dt_slice = 0.5
node_weights = ((5.0 / 24.0, 1.0 / 3.0, -1.0 / 24.0), (-1.0 / 24.0, 1.0 / 3.0, 5.0 / 24.0))
vmem_bytes = 52 << 20
source_rows = 18
moment_rows = 16


def high_part(value):
    return value.astype(bf16).astype(f32)


def parts_of(value, number):
    found = []
    for _ in range(number - 1):
        high = high_part(value)
        found.append(high)
        value = value - high
    found.append(high_part(value))
    return found


def norm_sq(rows):
    return rows[0:1] * rows[0:1] + rows[1:2] * rows[1:2] + rows[2:3] * rows[2:3]


def cross(a, b):
    return jnp.concatenate(
        [
            a[1:2] * b[2:3] - a[2:3] * b[1:2],
            a[2:3] * b[0:1] - a[0:1] * b[2:3],
            a[0:1] * b[1:2] - a[1:2] * b[0:1],
        ],
        0,
    )


def source_features(p):
    high, low = parts_of(p, 2)
    sq = parts_of(norm_sq(high + low), 3)
    one = jnp.ones_like(sq[0])
    return jnp.concatenate([high, high, low, low, *sq, one, one, one], 0).astype(bf16)


def target_features(x):
    high, low = parts_of(x, 2)
    sq = parts_of(norm_sq(high + low) + sigma_sq, 3)
    one = jnp.ones_like(sq[0])
    rows = [-2.0 * high, -2.0 * low, -2.0 * high, -2.0 * low, one, one, one, *sq]
    return jnp.concatenate(rows, 0).astype(bf16)


def source_moments(p, w):
    w = w * inv_four_pi
    pad = jnp.zeros((moment_rows - 12, p.shape[1]), f32)
    return jnp.concatenate([*parts_of(w, 2), *parts_of(cross(w, p), 2), pad], 0).astype(bf16)


def field(blocks, x, center, features, moments):
    width = x.shape[1]
    for number, (p, w) in enumerate(blocks):
        lanes = pl.ds(number * width, width)
        shifted = p - center
        features[:, lanes] = source_features(shifted)
        moments[:, lanes] = source_moments(shifted, w)
    x = x - center
    sq = lax.dot_general(
        features[...], target_features(x), (((0,), (0,)), ((), ())), preferred_element_type=f32
    )
    root = lax.rsqrt(sq)
    kernel = (root * root * root).astype(bf16)
    summed = jnp.dot(moments[...], kernel, preferred_element_type=f32)
    return cross(summed[0:3] + summed[3:6], x) - (summed[6:9] + summed[9:12])


def quad(row, a, b, c):
    return dt_slice * (row[0] * a + row[1] * b + row[2] * c)


def spread_out(ref, value):
    for number in range(ref.shape[0]):
        ref[number] = value


def nodes_kernel(all_ref, own_ref, velocity_ref, second_ref, send_ref, features, moments):
    halves, lines = all_ref.shape[:2]
    center = own_ref[0:3, 0:1]
    found = []
    for node in range(3):
        rows = pl.ds(3 * node, 3)
        blocks = [
            (all_ref[h, z, rows], all_ref[h, z, 9:12]) for z in range(lines) for h in range(halves)
        ]
        found.append(field(blocks, own_ref[rows], center, features, moments))
    velocity_ref[...] = jnp.concatenate(found, 0)
    second = own_ref[0:3] + quad(node_weights[0], *found)
    second_ref[...] = second
    spread_out(send_ref, second)


def swept_blocks(all_ref, gathered_ref):
    halves, lines = all_ref.shape[:2]
    return [
        (gathered_ref[halves * z + h], all_ref[h, z, 9:12])
        for z in range(lines)
        for h in range(halves)
    ]


def second_kernel(
    all_ref, gathered_ref, velocity_ref, second_ref, swept_ref, third_ref, send_ref, features, moments
):
    second = second_ref[...]
    blocks = swept_blocks(all_ref, gathered_ref)
    swept = field(blocks, second, second[:, 0:1], features, moments)
    swept_ref[...] = swept
    nodes = [velocity_ref[pl.ds(3 * node, 3)] for node in range(3)]
    third = second + 0.5 * dt_slice * (swept - nodes[1]) + quad(node_weights[1], *nodes)
    third_ref[...] = third
    spread_out(send_ref, third)


def third_kernel(
    all_ref, gathered_ref, velocity_ref, swept_ref, third_ref, send_ref, features, moments
):
    third = third_ref[...]
    blocks = swept_blocks(all_ref, gathered_ref)
    last = field(blocks, third, third[:, 0:1], features, moments)
    early = quad(node_weights[0], velocity_ref[0:3], swept_ref[...], last)
    late = quad(node_weights[1], velocity_ref[0:3], swept_ref[...], last)
    spread_out(send_ref, jnp.concatenate([early, early + late], 0))


def means_kernel(all_ref, second_ref, third_ref, quads_ref, coarse_ref, means_ref, send_ref, rows):
    halves, lines = all_ref.shape[:2]
    width = coarse_ref.shape[1]
    mine = jnp.broadcast_to(coarse_ref[...], (8, width)).T[:, 0:1]
    total = jnp.zeros((rows.shape[0], width), f32)
    for z in range(lines):
        for h in range(halves):
            number = halves * z + h
            values = jnp.concatenate(
                [all_ref[h, z, 0:3], second_ref[number], third_ref[number], quads_ref[number]], 0
            )
            ones = jnp.ones((3, width), f32)
            rows[...] = jnp.concatenate([*parts_of(values, 3), ones], 0).astype(bf16)
            same = jnp.where(mine == all_ref[h, z, 12:13], 1.0, 0.0).astype(bf16)
            total = total + lax.dot_general(
                rows[...], same, (((1,), (1,)), ((), ())), preferred_element_type=f32
            )
    means = (total[0:15] + total[15:30] + total[30:45]) / total[45:46]
    means_ref[...] = means
    first_slice = lax.axis_index("tm") == 0
    spread_out(send_ref, means[12:15] + jnp.where(first_slice, means[0:3], 0.0))


def ends_kernel(received_ref, means_ref, own_ref, second_ref, third_ref, fine_ref, end_ref):
    slice_index = lax.axis_index("tm")
    begin = jnp.where(slice_index == 0, means_ref[0:3], 0.0)
    for number in range(received_ref.shape[0]):
        begin = begin + jnp.where(number < slice_index, received_ref[number], 0.0)
    finish = begin + means_ref[12:15]
    fine_ref[0:3] = own_ref[0:3] + (begin - means_ref[0:3])
    fine_ref[3:6] = second_ref[...] + ((begin + means_ref[9:12]) - means_ref[3:6])
    fine_ref[6:9] = third_ref[...] + (finish - means_ref[6:9])
    width, half = finish.shape[1], end_ref.shape[1]
    even = lax.broadcasted_iota(jnp.int32, (width, half), 0) == 2 * lax.broadcasted_iota(
        jnp.int32, (width, half), 1
    )
    pick = jnp.where(even, 1.0, 0.0).astype(bf16)
    stacked = jnp.concatenate(parts_of(finish, 3), 0).astype(bf16)
    picked = jnp.dot(stacked, pick, preferred_element_type=f32)
    end_ref[...] = picked[0:3] + picked[3:6] + picked[6:9]


def call(kernel, shapes, scratch, *operands):
    return pl.pallas_call(
        kernel,
        out_shape=[jax.ShapeDtypeStruct(shape, f32) for shape in shapes],
        scratch_shapes=[pltpu.VMEM(shape, bf16) for shape in scratch],
        compiler_params=pltpu.CompilerParams(vmem_limit_bytes=vmem_bytes),
    )(*operands)


def body(node_pos, vorticity, coarse_of):
    width = vorticity.shape[1]
    domains = lax.axis_size("dom")
    slices = lax.axis_size("tm")
    own = node_pos.reshape(9, width)
    coarse = coarse_of.astype(f32)[None]
    block = jnp.concatenate([own, vorticity, coarse], 0)
    lines = domains // 2
    same_core = [[2 * z + h for z in range(lines)] for h in range(2)]
    same_chip = [[2 * z, 2 * z + 1] for z in range(lines)]
    along = lax.all_to_all(
        jnp.broadcast_to(block[None], (lines,) + block.shape),
        "dom",
        0,
        0,
        axis_index_groups=same_core,
    )
    everyone = lax.all_gather(along, "dom", axis=0, axis_index_groups=same_chip)
    count = domains * width
    scratch = [(source_rows, count), (moment_rows, count)]
    three = (3, width)
    velocity, second, send = call(
        nodes_kernel, [(9, width), three, (domains,) + three], scratch, everyone, own
    )
    seconds = lax.all_to_all(send, "dom", 0, 0)
    swept, third, send = call(
        second_kernel,
        [three, three, (domains,) + three],
        scratch,
        everyone,
        seconds,
        velocity,
        second,
    )
    thirds = lax.all_to_all(send, "dom", 0, 0)
    (send,) = call(
        third_kernel, [(domains, 6, width)], scratch, everyone, thirds, velocity, swept, third
    )
    quads = lax.all_to_all(send, "dom", 0, 0)
    means, send = call(
        means_kernel,
        [(15, width), (slices,) + three],
        [(48, width)],
        everyone,
        seconds,
        thirds,
        quads,
        coarse,
    )
    received = lax.all_to_all(send, "tm", 0, 0)
    fine_nodes, coarse_end = call(
        ends_kernel, [(9, width), (3, width // 2)], [], received, means, own, second, third
    )
    return fine_nodes.reshape(node_pos.shape), coarse_end[None]


def solution(mesh):
    return jax.shard_map(
        body,
        mesh=mesh,
        in_specs=(P("tm", None, None, "dom"), P(None, "dom"), P("dom")),
        out_specs=(P("tm", None, None, "dom"), P("tm", None, "dom")),
        check_vma=False,
    )
```

```python
import math

import jax
import jax.numpy as jnp
from jax import lax
from jax.experimental import pallas as pl
from jax.experimental.pallas import tpu as pltpu
from jax.sharding import PartitionSpec as P

f32 = jnp.float32
bf16 = jnp.bfloat16
inv_four_pi = 1.0 / (4.0 * math.pi)
sigma_sq = 0.01
dt_slice = 0.5
node_weights = ((5.0 / 24.0, 1.0 / 3.0, -1.0 / 24.0), (-1.0 / 24.0, 1.0 / 3.0, 5.0 / 24.0))
vmem_bytes = 52 << 20
source_rows = 18
moment_rows = 16


def high_part(value):
    return value.astype(bf16).astype(f32)


def parts_of(value, number):
    found = []
    for _ in range(number - 1):
        high = high_part(value)
        found.append(high)
        value = value - high
    found.append(high_part(value))
    return found


def norm_sq(rows):
    return rows[0:1] * rows[0:1] + rows[1:2] * rows[1:2] + rows[2:3] * rows[2:3]


def cross(a, b):
    return jnp.concatenate(
        [
            a[1:2] * b[2:3] - a[2:3] * b[1:2],
            a[2:3] * b[0:1] - a[0:1] * b[2:3],
            a[0:1] * b[1:2] - a[1:2] * b[0:1],
        ],
        0,
    )


def source_features(p):
    high, low = parts_of(p, 2)
    sq = parts_of(norm_sq(high + low), 3)
    one = jnp.ones_like(sq[0])
    return jnp.concatenate([high, high, low, low, *sq, one, one, one], 0).astype(bf16)


def target_features(x):
    high, low = parts_of(x, 2)
    sq = parts_of(norm_sq(high + low) + sigma_sq, 3)
    one = jnp.ones_like(sq[0])
    rows = [-2.0 * high, -2.0 * low, -2.0 * high, -2.0 * low, one, one, one, *sq]
    return jnp.concatenate(rows, 0).astype(bf16)


def source_moments(p, w):
    w = w * inv_four_pi
    pad = jnp.zeros((moment_rows - 12, p.shape[1]), f32)
    return jnp.concatenate([*parts_of(w, 2), *parts_of(cross(w, p), 2), pad], 0).astype(bf16)


def field(blocks, x, center, features, moments):
    width = x.shape[1]
    for number, (p, w) in enumerate(blocks):
        lanes = pl.ds(number * width, width)
        shifted = p - center
        features[:, lanes] = source_features(shifted)
        moments[:, lanes] = source_moments(shifted, w)
    x = x - center
    sq = lax.dot_general(
        features[...], target_features(x), (((0,), (0,)), ((), ())), preferred_element_type=f32
    )
    root = lax.rsqrt(sq)
    kernel = (root * root * root).astype(bf16)
    summed = jnp.dot(moments[...], kernel, preferred_element_type=f32)
    return cross(summed[0:3] + summed[3:6], x) - (summed[6:9] + summed[9:12])


def quad(row, a, b, c):
    return dt_slice * (row[0] * a + row[1] * b + row[2] * c)


lane = 128


def wide(ref, *index):
    return jnp.concatenate([ref[(*index, chunk)] for chunk in range(ref.shape[-2])], 1)


def store_chunks(ref, value):
    for chunk in range(ref.shape[-2]):
        ref[:, chunk] = value[:, chunk * lane : (chunk + 1) * lane]


def spread_out(ref, value):
    for number in range(ref.shape[0]):
        store_chunks(ref.at[number], value)


def prepare_kernel(nodes_ref, vorticity_ref, coarse_ref, own_ref, mine_ref, send_ref):
    own = nodes_ref[:, 0]
    mine = coarse_ref[...].astype(f32)
    own_ref[...] = own
    mine_ref[...] = mine
    spread_out(send_ref, jnp.concatenate([own, vorticity_ref[...], mine], 0))


def nodes_kernel(all_ref, own_ref, velocity_ref, second_ref, send_ref, features, moments):
    halves, lines = all_ref.shape[:2]
    center = own_ref[0:3, 0:1]
    found = []
    for node in range(3):
        rows = pl.ds(3 * node, 3)
        blocks = [
            (wide(all_ref, h, z, rows), wide(all_ref, h, z, pl.ds(9, 3)))
            for z in range(lines)
            for h in range(halves)
        ]
        found.append(field(blocks, own_ref[rows], center, features, moments))
    velocity_ref[...] = jnp.concatenate(found, 0)
    second = own_ref[0:3] + quad(node_weights[0], *found)
    second_ref[...] = second
    spread_out(send_ref, second)


def swept_blocks(all_ref, gathered_ref):
    halves, lines = all_ref.shape[:2]
    return [
        (wide(gathered_ref, halves * z + h, pl.ds(0, 3)), wide(all_ref, h, z, pl.ds(9, 3)))
        for z in range(lines)
        for h in range(halves)
    ]


def second_kernel(
    all_ref, gathered_ref, velocity_ref, second_ref, swept_ref, third_ref, send_ref, features, moments
):
    second = second_ref[...]
    blocks = swept_blocks(all_ref, gathered_ref)
    swept = field(blocks, second, second[:, 0:1], features, moments)
    swept_ref[...] = swept
    nodes = [velocity_ref[pl.ds(3 * node, 3)] for node in range(3)]
    third = second + 0.5 * dt_slice * (swept - nodes[1]) + quad(node_weights[1], *nodes)
    third_ref[...] = third
    spread_out(send_ref, third)


def third_kernel(
    all_ref, gathered_ref, velocity_ref, swept_ref, third_ref, send_ref, features, moments
):
    third = third_ref[...]
    blocks = swept_blocks(all_ref, gathered_ref)
    last = field(blocks, third, third[:, 0:1], features, moments)
    early = quad(node_weights[0], velocity_ref[0:3], swept_ref[...], last)
    late = quad(node_weights[1], velocity_ref[0:3], swept_ref[...], last)
    chunks = early.shape[1] // lane
    for number in range(send_ref.shape[0]):
        for chunk in range(chunks):
            lanes = slice(chunk * lane, (chunk + 1) * lane)
            send_ref[number, :, chunk] = early[:, lanes]
            send_ref[number, :, chunks + chunk] = (early + late)[:, lanes]


def means_kernel(all_ref, second_ref, third_ref, quads_ref, coarse_ref, means_ref, send_ref, rows):
    halves, lines = all_ref.shape[:2]
    width = coarse_ref.shape[1]
    chunks = width // lane
    mine = jnp.broadcast_to(coarse_ref[...], (8, width)).T[:, 0:1]
    total = jnp.zeros((rows.shape[0], width), f32)
    for z in range(lines):
        for h in range(halves):
            number = halves * z + h
            both = wide(quads_ref, number, pl.ds(0, 3))
            values = jnp.concatenate(
                [
                    wide(all_ref, h, z, pl.ds(0, 3)),
                    wide(second_ref, number, pl.ds(0, 3)),
                    wide(third_ref, number, pl.ds(0, 3)),
                    both[:, :width],
                    both[:, width:],
                ],
                0,
            )
            ones = jnp.ones((3, width), f32)
            rows[...] = jnp.concatenate([*parts_of(values, 3), ones], 0).astype(bf16)
            theirs = wide(all_ref, h, z, pl.ds(12, 1))
            same = jnp.where(mine == theirs, 1.0, 0.0).astype(bf16)
            total = total + lax.dot_general(
                rows[...], same, (((1,), (1,)), ((), ())), preferred_element_type=f32
            )
    means = (total[0:15] + total[15:30] + total[30:45]) / total[45:46]
    means_ref[...] = means
    first_slice = lax.axis_index("tm") == 0
    spread_out(send_ref, means[12:15] + jnp.where(first_slice, means[0:3], 0.0))


def ends_kernel(received_ref, means_ref, own_ref, second_ref, third_ref, fine_ref, end_ref):
    slice_index = lax.axis_index("tm")
    gathered = jnp.zeros(received_ref.shape[1:], f32)
    for number in range(received_ref.shape[0]):
        gathered = gathered + jnp.where(number < slice_index, received_ref[number], 0.0)
    gathered = jnp.concatenate([gathered[:, chunk] for chunk in range(gathered.shape[1])], 1)
    begin = jnp.where(slice_index == 0, means_ref[0:3], gathered)
    finish = begin + means_ref[12:15]
    fine_ref[0:3, 0] = own_ref[0:3] + (begin - means_ref[0:3])
    fine_ref[3:6, 0] = second_ref[...] + ((begin + means_ref[9:12]) - means_ref[3:6])
    fine_ref[6:9, 0] = third_ref[...] + (finish - means_ref[6:9])
    width, half = finish.shape[1], end_ref.shape[2]
    even = lax.broadcasted_iota(jnp.int32, (width, half), 0) == 2 * lax.broadcasted_iota(
        jnp.int32, (width, half), 1
    )
    pick = jnp.where(even, 1.0, 0.0).astype(bf16)
    stacked = jnp.concatenate(parts_of(finish, 3), 0).astype(bf16)
    picked = jnp.dot(stacked, pick, preferred_element_type=f32)
    end_ref[:, 0] = picked[0:3] + picked[3:6] + picked[6:9]


def call(kernel, shapes, scratch, *operands):
    return pl.pallas_call(
        kernel,
        out_shape=[jax.ShapeDtypeStruct(shape, f32) for shape in shapes],
        scratch_shapes=[pltpu.VMEM(shape, bf16) for shape in scratch],
        compiler_params=pltpu.CompilerParams(vmem_limit_bytes=vmem_bytes),
    )(*operands)


def body(node_pos, vorticity, coarse_of):
    width = vorticity.shape[1]
    domains = lax.axis_size("dom")
    slices = lax.axis_size("tm")
    lines = domains // 2
    chunks = width // lane
    same_core = [[2 * z + h for z in range(lines)] for h in range(2)]
    same_chip = [[2 * z, 2 * z + 1] for z in range(lines)]
    own, mine, send = call(
        prepare_kernel,
        [(9, width), (1, width), (lines, 13, chunks, lane)],
        [],
        node_pos.reshape(9, 1, width),
        vorticity,
        coarse_of[None],
    )
    along = lax.all_to_all(send, "dom", 0, 0, axis_index_groups=same_core)
    everyone = lax.all_gather(along, "dom", axis=0, axis_index_groups=same_chip)
    count = domains * width
    scratch = [(source_rows, count), (moment_rows, count)]
    three = (3, width)
    packed = (3, chunks, lane)
    velocity, second, send = call(
        nodes_kernel, [(9, width), three, (domains,) + packed], scratch, everyone, own
    )
    seconds = lax.all_to_all(send, "dom", 0, 0)
    swept, third, send = call(
        second_kernel,
        [three, three, (domains,) + packed],
        scratch,
        everyone,
        seconds,
        velocity,
        second,
    )
    thirds = lax.all_to_all(send, "dom", 0, 0)
    (send,) = call(
        third_kernel,
        [(domains, 3, 2 * chunks, lane)],
        scratch,
        everyone,
        thirds,
        velocity,
        swept,
        third,
    )
    quads = lax.all_to_all(send, "dom", 0, 0)
    means, send = call(
        means_kernel,
        [(15, width), (slices,) + packed],
        [(48, width)],
        everyone,
        seconds,
        thirds,
        quads,
        mine,
    )
    received = lax.all_to_all(send, "tm", 0, 0)
    fine_nodes, coarse_end = call(
        ends_kernel,
        [(9, 1, width), (3, 1, width // 2)],
        [],
        received,
        means,
        own,
        second,
        third,
    )
    return fine_nodes.reshape(node_pos.shape), coarse_end.reshape(1, 3, width // 2)


def solution(mesh):
    return jax.shard_map(
        body,
        mesh=mesh,
        in_specs=(P("tm", None, None, "dom"), P(None, "dom"), P("dom")),
        out_specs=(P("tm", None, None, "dom"), P("tm", None, "dom")),
        check_vma=False,
    )
```

```python
import math

import jax
import jax.numpy as jnp
from jax import lax
from jax.experimental import pallas as pl
from jax.experimental.pallas import tpu as pltpu
from jax.sharding import PartitionSpec as P

f32 = jnp.float32
bf16 = jnp.bfloat16
inv_four_pi = 1.0 / (4.0 * math.pi)
sigma_sq = 0.01
dt_slice = 0.5
node_weights = ((5.0 / 24.0, 1.0 / 3.0, -1.0 / 24.0), (-1.0 / 24.0, 1.0 / 3.0, 5.0 / 24.0))
vmem_bytes = 52 << 20
source_rows = 18
moment_rows = 16


def high_part(value):
    return value.astype(bf16).astype(f32)


def parts_of(value, number):
    found = []
    for _ in range(number - 1):
        high = high_part(value)
        found.append(high)
        value = value - high
    found.append(high_part(value))
    return found


def norm_sq(rows):
    return rows[0:1] * rows[0:1] + rows[1:2] * rows[1:2] + rows[2:3] * rows[2:3]


def cross(a, b):
    return jnp.concatenate(
        [
            a[1:2] * b[2:3] - a[2:3] * b[1:2],
            a[2:3] * b[0:1] - a[0:1] * b[2:3],
            a[0:1] * b[1:2] - a[1:2] * b[0:1],
        ],
        0,
    )


def source_features(p):
    high, low = parts_of(p, 2)
    sq = parts_of(norm_sq(high + low), 3)
    one = jnp.ones_like(sq[0])
    return jnp.concatenate([high, high, low, low, *sq, one, one, one], 0).astype(bf16)


def target_features(x):
    high, low = parts_of(x, 2)
    sq = parts_of(norm_sq(high + low) + sigma_sq, 3)
    one = jnp.ones_like(sq[0])
    rows = [-2.0 * high, -2.0 * low, -2.0 * high, -2.0 * low, one, one, one, *sq]
    return jnp.concatenate(rows, 0).astype(bf16)


def source_moments(p, w):
    w = w * inv_four_pi
    pad = jnp.zeros((moment_rows - 12, p.shape[1]), f32)
    return jnp.concatenate([*parts_of(w, 2), *parts_of(cross(w, p), 2), pad], 0).astype(bf16)


def field(blocks, x, center, features, moments):
    width = x.shape[1]
    for number, (p, w) in enumerate(blocks):
        lanes = pl.ds(number * width, width)
        shifted = p - center
        features[:, lanes] = source_features(shifted)
        moments[:, lanes] = source_moments(shifted, w)
    x = x - center
    sq = lax.dot_general(
        features[...], target_features(x), (((0,), (0,)), ((), ())), preferred_element_type=f32
    )
    root = lax.rsqrt(sq)
    kernel = (root * root * root).astype(bf16)
    summed = jnp.dot(moments[...], kernel, preferred_element_type=f32)
    return cross(summed[0:3] + summed[3:6], x) - (summed[6:9] + summed[9:12])


def quad(row, a, b, c):
    return dt_slice * (row[0] * a + row[1] * b + row[2] * c)


lane = 128


def wide(ref, *index):
    return jnp.concatenate([ref[(*index, chunk)] for chunk in range(ref.shape[-2])], 1)


def store_chunks(ref, value):
    for chunk in range(ref.shape[-2]):
        ref[:, chunk] = value[:, chunk * lane : (chunk + 1) * lane]


def spread_out(ref, value):
    for number in range(ref.shape[0]):
        store_chunks(ref.at[number], value)


def prepare_kernel(
    nodes_hbm,
    vorticity_hbm,
    coarse_hbm,
    own_ref,
    mine_ref,
    send_ref,
    nodes_ref,
    vorticity_ref,
    coarse_ref,
    arrived,
):
    pairs = [(nodes_hbm, nodes_ref), (vorticity_hbm, vorticity_ref), (coarse_hbm, coarse_ref)]
    copies = [
        pltpu.make_async_copy(source, target, arrived.at[number])
        for number, (source, target) in enumerate(pairs)
    ]
    for copy in copies:
        copy.start()
    for copy in copies:
        copy.wait()
    own = nodes_ref[:, 0]
    mine = coarse_ref[...].astype(f32)
    own_ref[...] = own
    mine_ref[...] = mine
    spread_out(send_ref, jnp.concatenate([own, vorticity_ref[...], mine], 0))


def nodes_kernel(all_ref, own_ref, velocity_ref, second_ref, send_ref, features, moments):
    halves, lines = all_ref.shape[:2]
    center = own_ref[0:3, 0:1]
    found = []
    for node in range(3):
        rows = pl.ds(3 * node, 3)
        blocks = [
            (wide(all_ref, h, z, rows), wide(all_ref, h, z, pl.ds(9, 3)))
            for z in range(lines)
            for h in range(halves)
        ]
        found.append(field(blocks, own_ref[rows], center, features, moments))
    velocity_ref[...] = jnp.concatenate(found, 0)
    second = own_ref[0:3] + quad(node_weights[0], *found)
    second_ref[...] = second
    spread_out(send_ref, second)


def swept_blocks(all_ref, gathered_ref):
    halves, lines = all_ref.shape[:2]
    return [
        (wide(gathered_ref, halves * z + h, pl.ds(0, 3)), wide(all_ref, h, z, pl.ds(9, 3)))
        for z in range(lines)
        for h in range(halves)
    ]


def second_kernel(
    all_ref, gathered_ref, velocity_ref, second_ref, swept_ref, third_ref, send_ref, features, moments
):
    second = second_ref[...]
    blocks = swept_blocks(all_ref, gathered_ref)
    swept = field(blocks, second, second[:, 0:1], features, moments)
    swept_ref[...] = swept
    nodes = [velocity_ref[pl.ds(3 * node, 3)] for node in range(3)]
    third = second + 0.5 * dt_slice * (swept - nodes[1]) + quad(node_weights[1], *nodes)
    third_ref[...] = third
    spread_out(send_ref, third)


def third_kernel(
    all_ref, gathered_ref, velocity_ref, swept_ref, third_ref, send_ref, features, moments
):
    third = third_ref[...]
    blocks = swept_blocks(all_ref, gathered_ref)
    last = field(blocks, third, third[:, 0:1], features, moments)
    early = quad(node_weights[0], velocity_ref[0:3], swept_ref[...], last)
    late = quad(node_weights[1], velocity_ref[0:3], swept_ref[...], last)
    chunks = early.shape[1] // lane
    for number in range(send_ref.shape[0]):
        for chunk in range(chunks):
            lanes = slice(chunk * lane, (chunk + 1) * lane)
            send_ref[number, :, chunk] = early[:, lanes]
            send_ref[number, :, chunks + chunk] = (early + late)[:, lanes]


def means_kernel(all_ref, second_ref, third_ref, quads_ref, mine_ref, means_ref, send_ref, rows):
    halves, lines = all_ref.shape[:2]
    width = mine_ref.shape[1]
    coarse = []
    for z in range(lines):
        for h in range(halves):
            number = halves * z + h
            both = wide(quads_ref, number, pl.ds(0, 3))
            values = jnp.concatenate(
                [
                    wide(all_ref, h, z, pl.ds(0, 3)),
                    wide(second_ref, number, pl.ds(0, 3)),
                    wide(third_ref, number, pl.ds(0, 3)),
                    both[:, :width],
                    both[:, width:],
                ],
                0,
            )
            ones = jnp.ones((3, width), f32)
            lanes = pl.ds(number * width, width)
            rows[:, lanes] = jnp.concatenate([*parts_of(values, 3), ones], 0).astype(bf16)
            coarse.append(all_ref[h, z, 12])
    columns = jnp.concatenate(coarse, 0).T
    columns = [columns[:, number : number + 1] for number in range(columns.shape[1])]
    mine = mine_ref[...]
    same = [jnp.where(column == mine, 1.0, 0.0).astype(bf16) for column in columns]
    total = jnp.dot(rows[...], jnp.concatenate(same, 0), preferred_element_type=f32)
    means = (total[0:15] + total[15:30] + total[30:45]) / total[45:46]
    means_ref[...] = means
    first_slice = lax.axis_index("tm") == 0
    spread_out(send_ref, means[12:15] + jnp.where(first_slice, means[0:3], 0.0))


def ends_kernel(received_ref, means_ref, own_ref, second_ref, third_ref, fine_ref, end_ref):
    slice_index = lax.axis_index("tm")
    gathered = jnp.zeros(received_ref.shape[1:], f32)
    for number in range(received_ref.shape[0]):
        gathered = gathered + jnp.where(number < slice_index, received_ref[number], 0.0)
    gathered = jnp.concatenate([gathered[:, chunk] for chunk in range(gathered.shape[1])], 1)
    begin = jnp.where(slice_index == 0, means_ref[0:3], gathered)
    finish = begin + means_ref[12:15]
    fine_ref[0:3, 0] = own_ref[0:3] + (begin - means_ref[0:3])
    fine_ref[3:6, 0] = second_ref[...] + ((begin + means_ref[9:12]) - means_ref[3:6])
    fine_ref[6:9, 0] = third_ref[...] + (finish - means_ref[6:9])
    width, half = finish.shape[1], end_ref.shape[2]
    even = lax.broadcasted_iota(jnp.int32, (width, half), 0) == 2 * lax.broadcasted_iota(
        jnp.int32, (width, half), 1
    )
    pick = jnp.where(even, 1.0, 0.0).astype(bf16)
    stacked = jnp.concatenate(parts_of(finish, 3), 0).astype(bf16)
    picked = jnp.dot(stacked, pick, preferred_element_type=f32)
    end_ref[:, 0] = picked[0:3] + picked[3:6] + picked[6:9]


def call(kernel, shapes, scratch, *operands):
    return pl.pallas_call(
        kernel,
        out_shape=[jax.ShapeDtypeStruct(shape, f32) for shape in shapes],
        scratch_shapes=[pltpu.VMEM(shape, bf16) for shape in scratch],
        compiler_params=pltpu.CompilerParams(vmem_limit_bytes=vmem_bytes),
    )(*operands)


def prepare(node_pos, vorticity, coarse_of, copies):
    width = vorticity.shape[1]
    nodes = node_pos.reshape(9, 1, width)
    coarse = coarse_of[None]
    shapes = [(9, width), (1, width), (copies, 13, width // lane, lane)]
    return pl.pallas_call(
        prepare_kernel,
        out_shape=[jax.ShapeDtypeStruct(shape, f32) for shape in shapes],
        in_specs=[pl.BlockSpec(memory_space=pltpu.HBM)] * 3,
        scratch_shapes=[
            pltpu.VMEM(nodes.shape, f32),
            pltpu.VMEM(vorticity.shape, f32),
            pltpu.VMEM(coarse.shape, jnp.int32),
            pltpu.SemaphoreType.DMA((3,)),
        ],
    )(nodes, vorticity, coarse)


def body(node_pos, vorticity, coarse_of):
    width = vorticity.shape[1]
    domains = lax.axis_size("dom")
    slices = lax.axis_size("tm")
    lines = domains // 2
    chunks = width // lane
    same_core = [[2 * z + h for z in range(lines)] for h in range(2)]
    same_chip = [[2 * z, 2 * z + 1] for z in range(lines)]
    own, mine, send = prepare(node_pos, vorticity, coarse_of, lines)
    along = lax.all_to_all(send, "dom", 0, 0, axis_index_groups=same_core)
    everyone = lax.all_gather(along, "dom", axis=0, axis_index_groups=same_chip)
    count = domains * width
    scratch = [(source_rows, count), (moment_rows, count)]
    three = (3, width)
    packed = (3, chunks, lane)
    velocity, second, send = call(
        nodes_kernel, [(9, width), three, (domains,) + packed], scratch, everyone, own
    )
    seconds = lax.all_to_all(send, "dom", 0, 0)
    swept, third, send = call(
        second_kernel,
        [three, three, (domains,) + packed],
        scratch,
        everyone,
        seconds,
        velocity,
        second,
    )
    thirds = lax.all_to_all(send, "dom", 0, 0)
    (send,) = call(
        third_kernel,
        [(domains, 3, 2 * chunks, lane)],
        scratch,
        everyone,
        thirds,
        velocity,
        swept,
        third,
    )
    quads = lax.all_to_all(send, "dom", 0, 0)
    means, send = call(
        means_kernel,
        [(15, width), (slices,) + packed],
        [(48, count)],
        everyone,
        seconds,
        thirds,
        quads,
        mine,
    )
    received = lax.all_to_all(send, "tm", 0, 0)
    fine_nodes, coarse_end = call(
        ends_kernel,
        [(9, 1, width), (3, 1, width // 2)],
        [],
        received,
        means,
        own,
        second,
        third,
    )
    return fine_nodes.reshape(node_pos.shape), coarse_end.reshape(1, 3, width // 2)


def solution(mesh):
    return jax.shard_map(
        body,
        mesh=mesh,
        in_specs=(P("tm", None, None, "dom"), P(None, "dom"), P("dom")),
        out_specs=(P("tm", None, None, "dom"), P("tm", None, "dom")),
        check_vma=False,
    )
```

```python
import math

import jax
import jax.numpy as jnp
from jax import lax
from jax.experimental import pallas as pl
from jax.experimental.pallas import tpu as pltpu
from jax.sharding import PartitionSpec as P

f32 = jnp.float32
bf16 = jnp.bfloat16
inv_four_pi = 1.0 / (4.0 * math.pi)
sigma_sq = 0.01
dt_slice = 0.5
node_weights = ((5.0 / 24.0, 1.0 / 3.0, -1.0 / 24.0), (-1.0 / 24.0, 1.0 / 3.0, 5.0 / 24.0))
vmem_bytes = 52 << 20
source_rows = 18
moment_rows = 16


def high_part(value):
    return value.astype(bf16).astype(f32)


def parts_of(value, number):
    found = []
    for _ in range(number - 1):
        high = high_part(value)
        found.append(high)
        value = value - high
    found.append(high_part(value))
    return found


def norm_sq(rows):
    return rows[0:1] * rows[0:1] + rows[1:2] * rows[1:2] + rows[2:3] * rows[2:3]


def cross(a, b):
    return jnp.concatenate(
        [
            a[1:2] * b[2:3] - a[2:3] * b[1:2],
            a[2:3] * b[0:1] - a[0:1] * b[2:3],
            a[0:1] * b[1:2] - a[1:2] * b[0:1],
        ],
        0,
    )


def source_features(p):
    high, low = parts_of(p, 2)
    sq = parts_of(norm_sq(high + low), 3)
    one = jnp.ones_like(sq[0])
    return jnp.concatenate([high, high, low, low, *sq, one, one, one], 0).astype(bf16)


def target_features(x):
    high, low = parts_of(x, 2)
    sq = parts_of(norm_sq(high + low) + sigma_sq, 3)
    one = jnp.ones_like(sq[0])
    rows = [-2.0 * high, -2.0 * low, -2.0 * high, -2.0 * low, one, one, one, *sq]
    return jnp.concatenate(rows, 0).astype(bf16)


def source_moments(p, w):
    w = w * inv_four_pi
    pad = jnp.zeros((moment_rows - 12, p.shape[1]), f32)
    return jnp.concatenate([*parts_of(w, 2), *parts_of(cross(w, p), 2), pad], 0).astype(bf16)


def field(blocks, x, center, features, moments):
    width = x.shape[1]
    for number, (p, w) in enumerate(blocks):
        lanes = pl.ds(number * width, width)
        shifted = p - center
        features[:, lanes] = source_features(shifted)
        moments[:, lanes] = source_moments(shifted, w)
    x = x - center
    sq = lax.dot_general(
        features[...], target_features(x), (((0,), (0,)), ((), ())), preferred_element_type=f32
    )
    root = lax.rsqrt(sq)
    kernel = (root * root * root).astype(bf16)
    summed = jnp.dot(moments[...], kernel, preferred_element_type=f32)
    return cross(summed[0:3] + summed[3:6], x) - (summed[6:9] + summed[9:12])


def quad(row, a, b, c):
    return dt_slice * (row[0] * a + row[1] * b + row[2] * c)


lane = 128


def wide(ref, *index):
    return jnp.concatenate([ref[(*index, chunk)] for chunk in range(ref.shape[-2])], 1)


def store_chunks(ref, value):
    for chunk in range(ref.shape[-2]):
        ref[:, chunk] = value[:, chunk * lane : (chunk + 1) * lane]


def spread_out(ref, value):
    for number in range(ref.shape[0]):
        store_chunks(ref.at[number], value)


def prepare_kernel(
    nodes_hbm,
    vorticity_hbm,
    coarse_hbm,
    own_ref,
    mine_ref,
    send_ref,
    nodes_ref,
    vorticity_ref,
    coarse_ref,
    arrived,
):
    pairs = [(nodes_hbm, nodes_ref), (vorticity_hbm, vorticity_ref), (coarse_hbm, coarse_ref)]
    copies = [
        pltpu.make_async_copy(source, target, arrived.at[number])
        for number, (source, target) in enumerate(pairs)
    ]
    for copy in copies:
        copy.start()
    for copy in copies:
        copy.wait()
    own = nodes_ref[:, 0]
    mine = coarse_ref[...].astype(f32)
    own_ref[...] = own
    mine_ref[...] = mine
    spread_out(send_ref, jnp.concatenate([own, vorticity_ref[...], mine], 0))


def nodes_kernel(all_ref, own_ref, velocity_ref, second_ref, send_ref, features, moments):
    halves, lines = all_ref.shape[:2]
    center = own_ref[0:3, 0:1]
    found = []
    for node in range(3):
        rows = pl.ds(3 * node, 3)
        blocks = [
            (wide(all_ref, h, z, rows), wide(all_ref, h, z, pl.ds(9, 3)))
            for z in range(lines)
            for h in range(halves)
        ]
        found.append(field(blocks, own_ref[rows], center, features, moments))
    velocity_ref[...] = jnp.concatenate(found, 0)
    second = own_ref[0:3] + quad(node_weights[0], *found)
    second_ref[...] = second
    spread_out(send_ref, second)


def swept_blocks(all_ref, gathered_ref):
    halves, lines = all_ref.shape[:2]
    return [
        (wide(gathered_ref, halves * z + h, pl.ds(0, 3)), wide(all_ref, h, z, pl.ds(9, 3)))
        for z in range(lines)
        for h in range(halves)
    ]


def second_kernel(
    all_ref, gathered_ref, velocity_ref, second_ref, swept_ref, third_ref, send_ref, features, moments
):
    second = second_ref[...]
    blocks = swept_blocks(all_ref, gathered_ref)
    swept = field(blocks, second, second[:, 0:1], features, moments)
    swept_ref[...] = swept
    nodes = [velocity_ref[pl.ds(3 * node, 3)] for node in range(3)]
    third = second + 0.5 * dt_slice * (swept - nodes[1]) + quad(node_weights[1], *nodes)
    third_ref[...] = third
    spread_out(send_ref, third)


def third_kernel(
    all_ref, gathered_ref, velocity_ref, swept_ref, third_ref, send_ref, features, moments
):
    third = third_ref[...]
    blocks = swept_blocks(all_ref, gathered_ref)
    last = field(blocks, third, third[:, 0:1], features, moments)
    early = quad(node_weights[0], velocity_ref[0:3], swept_ref[...], last)
    late = quad(node_weights[1], velocity_ref[0:3], swept_ref[...], last)
    chunks = early.shape[1] // lane
    for number in range(send_ref.shape[0]):
        for chunk in range(chunks):
            lanes = slice(chunk * lane, (chunk + 1) * lane)
            send_ref[number, :, chunk] = early[:, lanes]
            send_ref[number, :, chunks + chunk] = (early + late)[:, lanes]


def means_kernel(all_ref, second_ref, third_ref, quads_ref, mine_ref, means_ref, send_ref, rows):
    halves, lines = all_ref.shape[:2]
    width = mine_ref.shape[1]
    coarse = []
    for z in range(lines):
        for h in range(halves):
            number = halves * z + h
            both = wide(quads_ref, number, pl.ds(0, 3))
            values = jnp.concatenate(
                [
                    wide(all_ref, h, z, pl.ds(0, 3)),
                    wide(second_ref, number, pl.ds(0, 3)),
                    wide(third_ref, number, pl.ds(0, 3)),
                    both[:, :width],
                    both[:, width:],
                ],
                0,
            )
            ones = jnp.ones((3, width), f32)
            lanes = pl.ds(number * width, width)
            rows[:, lanes] = jnp.concatenate([*parts_of(values, 3), ones], 0).astype(bf16)
            coarse.append(all_ref[h, z, 12])
    columns = jnp.concatenate(coarse, 0).T
    columns = [columns[:, number : number + 1] for number in range(columns.shape[1])]
    mine = mine_ref[...]
    same = [jnp.where(column == mine, 1.0, 0.0).astype(bf16) for column in columns]
    total = jnp.dot(rows[...], jnp.concatenate(same, 0), preferred_element_type=f32)
    means = (total[0:15] + total[15:30] + total[30:45]) / total[45:46]
    means_ref[...] = means
    first_slice = lax.axis_index("tm") == 0
    spread_out(send_ref, means[12:15] + jnp.where(first_slice, means[0:3], 0.0))


def ends_kernel(received_ref, means_ref, own_ref, second_ref, third_ref, fine_ref, end_ref):
    slice_index = lax.axis_index("tm")
    gathered = jnp.zeros(received_ref.shape[1:], f32)
    for number in range(received_ref.shape[0]):
        gathered = gathered + jnp.where(number < slice_index, received_ref[number], 0.0)
    gathered = jnp.concatenate([gathered[:, chunk] for chunk in range(gathered.shape[1])], 1)
    begin = jnp.where(slice_index == 0, means_ref[0:3], gathered)
    finish = begin + means_ref[12:15]
    fine_ref[0:3, 0] = own_ref[0:3] + (begin - means_ref[0:3])
    fine_ref[3:6, 0] = second_ref[...] + ((begin + means_ref[9:12]) - means_ref[3:6])
    fine_ref[6:9, 0] = third_ref[...] + (finish - means_ref[6:9])
    width, half = finish.shape[1], end_ref.shape[2]
    even = lax.broadcasted_iota(jnp.int32, (width, half), 0) == 2 * lax.broadcasted_iota(
        jnp.int32, (width, half), 1
    )
    pick = jnp.where(even, 1.0, 0.0).astype(bf16)
    stacked = jnp.concatenate(parts_of(finish, 3), 0).astype(bf16)
    picked = jnp.dot(stacked, pick, preferred_element_type=f32)
    end_ref[:, 0] = picked[0:3] + picked[3:6] + picked[6:9]


def call(kernel, shapes, scratch, *operands):
    return pl.pallas_call(
        kernel,
        out_shape=[jax.ShapeDtypeStruct(shape, f32) for shape in shapes],
        scratch_shapes=[pltpu.VMEM(shape, bf16) for shape in scratch],
        compiler_params=pltpu.CompilerParams(vmem_limit_bytes=vmem_bytes),
    )(*operands)


def prepare(node_pos, vorticity, coarse_of, copies):
    width = vorticity.shape[1]
    nodes = node_pos.reshape(9, 1, width)
    coarse = coarse_of[None]
    shapes = [(9, width), (1, width), (copies, 13, width // lane, lane)]
    return pl.pallas_call(
        prepare_kernel,
        out_shape=[jax.ShapeDtypeStruct(shape, f32) for shape in shapes],
        in_specs=[pl.BlockSpec(memory_space=pltpu.HBM)] * 3,
        scratch_shapes=[
            pltpu.VMEM(nodes.shape, f32),
            pltpu.VMEM(vorticity.shape, f32),
            pltpu.VMEM(coarse.shape, jnp.int32),
            pltpu.SemaphoreType.DMA((3,)),
        ],
        compiler_params=pltpu.CompilerParams(vmem_limit_bytes=vmem_bytes),
    )(*[pltpu.with_memory_space_constraint(x, pltpu.HBM) for x in (nodes, vorticity, coarse)])


def body(node_pos, vorticity, coarse_of):
    width = vorticity.shape[1]
    domains = lax.axis_size("dom")
    slices = lax.axis_size("tm")
    lines = domains // 2
    chunks = width // lane
    same_core = [[2 * z + h for z in range(lines)] for h in range(2)]
    same_chip = [[2 * z, 2 * z + 1] for z in range(lines)]
    own, mine, send = prepare(node_pos, vorticity, coarse_of, lines)
    along = lax.all_to_all(send, "dom", 0, 0, axis_index_groups=same_core)
    everyone = lax.all_gather(along, "dom", axis=0, axis_index_groups=same_chip)
    count = domains * width
    scratch = [(source_rows, count), (moment_rows, count)]
    three = (3, width)
    packed = (3, chunks, lane)
    velocity, second, send = call(
        nodes_kernel, [(9, width), three, (domains,) + packed], scratch, everyone, own
    )
    seconds = lax.all_to_all(send, "dom", 0, 0)
    swept, third, send = call(
        second_kernel,
        [three, three, (domains,) + packed],
        scratch,
        everyone,
        seconds,
        velocity,
        second,
    )
    thirds = lax.all_to_all(send, "dom", 0, 0)
    (send,) = call(
        third_kernel,
        [(domains, 3, 2 * chunks, lane)],
        scratch,
        everyone,
        thirds,
        velocity,
        swept,
        third,
    )
    quads = lax.all_to_all(send, "dom", 0, 0)
    means, send = call(
        means_kernel,
        [(15, width), (slices,) + packed],
        [(48, count)],
        everyone,
        seconds,
        thirds,
        quads,
        mine,
    )
    received = lax.all_to_all(send, "tm", 0, 0)
    fine_nodes, coarse_end = call(
        ends_kernel,
        [(9, 1, width), (3, 1, width // 2)],
        [],
        received,
        means,
        own,
        second,
        third,
    )
    return fine_nodes.reshape(node_pos.shape), coarse_end.reshape(1, 3, width // 2)


def solution(mesh):
    return jax.shard_map(
        body,
        mesh=mesh,
        in_specs=(P("tm", None, None, "dom"), P(None, "dom"), P("dom")),
        out_specs=(P("tm", None, None, "dom"), P("tm", None, "dom")),
        check_vma=False,
    )
```

```python
import math

import jax
import jax.numpy as jnp
from jax import lax
from jax.experimental import pallas as pl
from jax.experimental.pallas import tpu as pltpu
from jax.sharding import PartitionSpec as P

f32 = jnp.float32
bf16 = jnp.bfloat16
inv_four_pi = 1.0 / (4.0 * math.pi)
sigma_sq = 0.01
dt_slice = 0.5
node_weights = ((5.0 / 24.0, 1.0 / 3.0, -1.0 / 24.0), (-1.0 / 24.0, 1.0 / 3.0, 5.0 / 24.0))
vmem_bytes = 52 << 20
part_blocks = 2
rows_cycle = 8


def high_part(value):
    return value.astype(bf16).astype(f32)


def parts_of(value, number):
    found = []
    for _ in range(number - 1):
        high = high_part(value)
        found.append(high)
        value = value - high
    found.append(high_part(value))
    return found


def norm_sq(rows):
    return rows[0:1] * rows[0:1] + rows[1:2] * rows[1:2] + rows[2:3] * rows[2:3]


def cross(a, b):
    return jnp.concatenate(
        [
            a[1:2] * b[2:3] - a[2:3] * b[1:2],
            a[2:3] * b[0:1] - a[0:1] * b[2:3],
            a[0:1] * b[1:2] - a[1:2] * b[0:1],
        ],
        0,
    )


def cyclic(rows):
    return jnp.concatenate([rows, rows, rows[0:2]], 0)


def rotated(rows, number):
    return pltpu.roll(rows, rows_cycle - number, 0)


def source_rows(p, w, leading):
    w = w * inv_four_pi
    high, low = parts_of(p, 2)
    near = jnp.where(leading, high, low)
    summed = high + low
    first, second, third = parts_of(summed * summed, 3)
    norms = jnp.where(leading, first, second)
    last = jnp.where(leading, third, 1.0)
    features = jnp.concatenate([near, near, norms, last], 0).astype(bf16)
    high, low = parts_of(w, 2)
    strengths = jnp.where(leading, high, low)
    products = jnp.where(leading, rotated(w, 1), rotated(w, 2)) * jnp.where(
        leading, rotated(p, 2), rotated(p, 1)
    )
    crossed = products - jnp.where(leading, rotated(products, 3), rotated(products, 5))
    high, low = parts_of(crossed, 2)
    moments = jnp.concatenate([strengths, jnp.where(leading, high, low)], 0).astype(bf16)
    return features, moments


def target_rows(x):
    high, low = parts_of(x, 2)
    norms = parts_of(norm_sq(high + low) + sigma_sq, 3)
    none = jnp.zeros((2, x.shape[1]), f32)
    one = jnp.ones_like(x)
    high, low = -2.0 * high, -2.0 * low
    rows = [high, high, none, low, low, none, one, one, none, one, *norms, none]
    return jnp.concatenate(rows, 0).astype(bf16)


def field(blocks, x, center):
    width = x.shape[1]
    leading = lax.broadcasted_iota(jnp.int32, (rows_cycle, width), 0) < 3
    centers = cyclic(jnp.broadcast_to(center, x.shape))
    x = x - center
    targets = target_rows(x)
    total = jnp.zeros((2 * rows_cycle, width), f32)
    for begin in range(0, len(blocks), part_blocks):
        rows = [
            source_rows(cyclic(p) - centers, cyclic(w), leading)
            for p, w in blocks[begin : begin + part_blocks]
        ]
        features = jnp.concatenate([pair[0] for pair in rows], 1)
        moments = jnp.concatenate([pair[1] for pair in rows], 1)
        sq = lax.dot_general(
            features, targets, (((0,), (0,)), ((), ())), preferred_element_type=f32
        )
        root = lax.rsqrt(sq)
        kernel = (root * root * root).astype(bf16)
        total = total + jnp.dot(moments, kernel, preferred_element_type=f32)
    return cross(total[0:3] + total[3:6], x) - (total[8:11] - total[11:14])


def quad(row, a, b, c):
    return dt_slice * (row[0] * a + row[1] * b + row[2] * c)


lane = 128


def wide(ref, *index):
    return jnp.concatenate([ref[(*index, chunk)] for chunk in range(ref.shape[-2])], 1)


def store_chunks(ref, value):
    for chunk in range(ref.shape[-2]):
        ref[:, chunk] = value[:, chunk * lane : (chunk + 1) * lane]


def spread_out(ref, value):
    for number in range(ref.shape[0]):
        store_chunks(ref.at[number], value)


def prepare_kernel(
    nodes_hbm,
    vorticity_hbm,
    coarse_hbm,
    own_ref,
    mine_ref,
    send_ref,
    nodes_ref,
    vorticity_ref,
    coarse_ref,
    arrived,
):
    pairs = [(nodes_hbm, nodes_ref), (vorticity_hbm, vorticity_ref), (coarse_hbm, coarse_ref)]
    copies = [
        pltpu.make_async_copy(source, target, arrived.at[number])
        for number, (source, target) in enumerate(pairs)
    ]
    for copy in copies:
        copy.start()
    for copy in copies:
        copy.wait()
    own = nodes_ref[:, 0]
    mine = coarse_ref[...].astype(f32)
    own_ref[...] = own
    mine_ref[...] = mine
    spread_out(send_ref, jnp.concatenate([own, vorticity_ref[...], mine], 0))


def nodes_kernel(all_ref, own_ref, velocity_ref, second_ref, send_ref):
    halves, lines = all_ref.shape[:2]
    center = own_ref[0:3, 0:1]
    found = []
    for node in range(3):
        rows = pl.ds(3 * node, 3)
        blocks = [
            (wide(all_ref, h, z, rows), wide(all_ref, h, z, pl.ds(9, 3)))
            for z in range(lines)
            for h in range(halves)
        ]
        found.append(field(blocks, own_ref[rows], center))
    velocity_ref[...] = jnp.concatenate(found, 0)
    second = own_ref[0:3] + quad(node_weights[0], *found)
    second_ref[...] = second
    spread_out(send_ref, second)


def swept_blocks(all_ref, gathered_ref):
    halves, lines = all_ref.shape[:2]
    return [
        (wide(gathered_ref, halves * z + h, pl.ds(0, 3)), wide(all_ref, h, z, pl.ds(9, 3)))
        for z in range(lines)
        for h in range(halves)
    ]


def second_kernel(
    all_ref, gathered_ref, velocity_ref, second_ref, swept_ref, third_ref, send_ref
):
    second = second_ref[...]
    blocks = swept_blocks(all_ref, gathered_ref)
    swept = field(blocks, second, second[:, 0:1])
    swept_ref[...] = swept
    nodes = [velocity_ref[pl.ds(3 * node, 3)] for node in range(3)]
    third = second + 0.5 * dt_slice * (swept - nodes[1]) + quad(node_weights[1], *nodes)
    third_ref[...] = third
    spread_out(send_ref, third)


def third_kernel(
    all_ref, gathered_ref, velocity_ref, swept_ref, third_ref, send_ref
):
    third = third_ref[...]
    blocks = swept_blocks(all_ref, gathered_ref)
    last = field(blocks, third, third[:, 0:1])
    early = quad(node_weights[0], velocity_ref[0:3], swept_ref[...], last)
    late = quad(node_weights[1], velocity_ref[0:3], swept_ref[...], last)
    chunks = early.shape[1] // lane
    for number in range(send_ref.shape[0]):
        for chunk in range(chunks):
            lanes = slice(chunk * lane, (chunk + 1) * lane)
            send_ref[number, :, chunk] = early[:, lanes]
            send_ref[number, :, chunks + chunk] = (early + late)[:, lanes]


def means_kernel(all_ref, second_ref, third_ref, quads_ref, mine_ref, means_ref, send_ref):
    halves, lines = all_ref.shape[:2]
    width = mine_ref.shape[1]
    ones = jnp.ones((3, width), f32)
    rows, coarse = [], []
    for z in range(lines):
        for h in range(halves):
            number = halves * z + h
            both = wide(quads_ref, number, pl.ds(0, 3))
            values = jnp.concatenate(
                [
                    wide(all_ref, h, z, pl.ds(0, 3)),
                    wide(second_ref, number, pl.ds(0, 3)),
                    wide(third_ref, number, pl.ds(0, 3)),
                    both[:, :width],
                    both[:, width:],
                ],
                0,
            )
            rows.append(jnp.concatenate([*parts_of(values, 3), ones], 0).astype(bf16))
            coarse.append(all_ref[h, z, 12])
    columns = jnp.concatenate(coarse, 0).T
    mine = mine_ref[...]
    total = jnp.zeros((48, width), f32)
    for begin in range(0, len(rows), 2 * part_blocks):
        end = begin + 2 * part_blocks
        chunks = range(begin * width // lane, end * width // lane)
        same = [
            jnp.where(columns[:, chunk : chunk + 1] == mine, 1.0, 0.0).astype(bf16)
            for chunk in chunks
        ]
        total = total + jnp.dot(
            jnp.concatenate(rows[begin:end], 1),
            jnp.concatenate(same, 0),
            preferred_element_type=f32,
        )
    means = (total[0:15] + total[15:30] + total[30:45]) / total[45:46]
    means_ref[...] = means
    first_slice = lax.axis_index("tm") == 0
    spread_out(send_ref, means[12:15] + jnp.where(first_slice, means[0:3], 0.0))


def ends_kernel(received_ref, means_ref, own_ref, second_ref, third_ref, fine_ref, end_ref):
    slice_index = lax.axis_index("tm")
    gathered = jnp.zeros(received_ref.shape[1:], f32)
    for number in range(received_ref.shape[0]):
        gathered = gathered + jnp.where(number < slice_index, received_ref[number], 0.0)
    gathered = jnp.concatenate([gathered[:, chunk] for chunk in range(gathered.shape[1])], 1)
    begin = jnp.where(slice_index == 0, means_ref[0:3], gathered)
    finish = begin + means_ref[12:15]
    fine_ref[0:3, 0] = own_ref[0:3] + (begin - means_ref[0:3])
    fine_ref[3:6, 0] = second_ref[...] + ((begin + means_ref[9:12]) - means_ref[3:6])
    fine_ref[6:9, 0] = third_ref[...] + (finish - means_ref[6:9])
    width, half = finish.shape[1], end_ref.shape[2]
    even = lax.broadcasted_iota(jnp.int32, (width, half), 0) == 2 * lax.broadcasted_iota(
        jnp.int32, (width, half), 1
    )
    pick = jnp.where(even, 1.0, 0.0).astype(bf16)
    stacked = jnp.concatenate(parts_of(finish, 3), 0).astype(bf16)
    picked = jnp.dot(stacked, pick, preferred_element_type=f32)
    end_ref[:, 0] = picked[0:3] + picked[3:6] + picked[6:9]


def call(kernel, shapes, *operands):
    return pl.pallas_call(
        kernel,
        out_shape=[jax.ShapeDtypeStruct(shape, f32) for shape in shapes],
        compiler_params=pltpu.CompilerParams(vmem_limit_bytes=vmem_bytes),
    )(*operands)


def prepare(node_pos, vorticity, coarse_of, copies):
    width = vorticity.shape[1]
    nodes = node_pos.reshape(9, 1, width)
    coarse = coarse_of[None]
    shapes = [(9, width), (1, width), (copies, 13, width // lane, lane)]
    return pl.pallas_call(
        prepare_kernel,
        out_shape=[jax.ShapeDtypeStruct(shape, f32) for shape in shapes],
        in_specs=[pl.BlockSpec(memory_space=pltpu.HBM)] * 3,
        scratch_shapes=[
            pltpu.VMEM(nodes.shape, f32),
            pltpu.VMEM(vorticity.shape, f32),
            pltpu.VMEM(coarse.shape, jnp.int32),
            pltpu.SemaphoreType.DMA((3,)),
        ],
        compiler_params=pltpu.CompilerParams(vmem_limit_bytes=vmem_bytes),
    )(*[pltpu.with_memory_space_constraint(x, pltpu.HBM) for x in (nodes, vorticity, coarse)])


def body(node_pos, vorticity, coarse_of):
    width = vorticity.shape[1]
    domains = lax.axis_size("dom")
    slices = lax.axis_size("tm")
    lines = domains // 2
    chunks = width // lane
    same_core = [[2 * z + h for z in range(lines)] for h in range(2)]
    same_chip = [[2 * z, 2 * z + 1] for z in range(lines)]
    own, mine, send = prepare(node_pos, vorticity, coarse_of, lines)
    along = lax.all_to_all(send, "dom", 0, 0, axis_index_groups=same_core)
    everyone = lax.all_gather(along, "dom", axis=0, axis_index_groups=same_chip)
    three = (3, width)
    packed = (3, chunks, lane)
    velocity, second, send = call(
        nodes_kernel, [(9, width), three, (domains,) + packed], everyone, own
    )
    seconds = lax.all_to_all(send, "dom", 0, 0)
    swept, third, send = call(
        second_kernel,
        [three, three, (domains,) + packed],
        everyone,
        seconds,
        velocity,
        second,
    )
    thirds = lax.all_to_all(send, "dom", 0, 0)
    (send,) = call(
        third_kernel,
        [(domains, 3, 2 * chunks, lane)],
        everyone,
        thirds,
        velocity,
        swept,
        third,
    )
    quads = lax.all_to_all(send, "dom", 0, 0)
    means, send = call(
        means_kernel,
        [(15, width), (slices,) + packed],
        everyone,
        seconds,
        thirds,
        quads,
        mine,
    )
    received = lax.all_to_all(send, "tm", 0, 0)
    fine_nodes, coarse_end = call(
        ends_kernel,
        [(9, 1, width), (3, 1, width // 2)],
        received,
        means,
        own,
        second,
        third,
    )
    return fine_nodes.reshape(node_pos.shape), coarse_end.reshape(1, 3, width // 2)


def solution(mesh):
    return jax.shard_map(
        body,
        mesh=mesh,
        in_specs=(P("tm", None, None, "dom"), P(None, "dom"), P("dom")),
        out_specs=(P("tm", None, None, "dom"), P("tm", None, "dom")),
        check_vma=False,
    )
```

```python
import math

import jax
import jax.numpy as jnp
from jax import lax
from jax.experimental import pallas as pl
from jax.experimental.pallas import tpu as pltpu
from jax.sharding import PartitionSpec as P

f32 = jnp.float32
bf16 = jnp.bfloat16
inv_four_pi = 1.0 / (4.0 * math.pi)
sigma_sq = 0.01
dt_slice = 0.5
node_weights = ((5.0 / 24.0, 1.0 / 3.0, -1.0 / 24.0), (-1.0 / 24.0, 1.0 / 3.0, 5.0 / 24.0))
vmem_bytes = 52 << 20
part_blocks = 2
rows_cycle = 8


def high_part(value):
    return value.astype(bf16).astype(f32)


def parts_of(value, number):
    found = []
    for _ in range(number - 1):
        high = high_part(value)
        found.append(high)
        value = value - high
    found.append(high_part(value))
    return found


def norm_sq(rows):
    return rows[0:1] * rows[0:1] + rows[1:2] * rows[1:2] + rows[2:3] * rows[2:3]


def cross(a, b):
    return jnp.concatenate(
        [
            a[1:2] * b[2:3] - a[2:3] * b[1:2],
            a[2:3] * b[0:1] - a[0:1] * b[2:3],
            a[0:1] * b[1:2] - a[1:2] * b[0:1],
        ],
        0,
    )


def cyclic(rows):
    return jnp.concatenate([rows, rows, rows[0:2]], 0)


def rotated(rows, number):
    return pltpu.roll(rows, rows_cycle - number, 0)


def source_rows(p, w, leading):
    w = w * inv_four_pi
    high, low = parts_of(p, 2)
    near = jnp.where(leading, high, low)
    summed = high + low
    first, second, third = parts_of(summed * summed, 3)
    norms = jnp.where(leading, first, second)
    last = jnp.where(leading, third, 1.0)
    features = jnp.concatenate([near, near, norms, last], 0).astype(bf16)
    high, low = parts_of(w, 2)
    strengths = jnp.where(leading, high, low)
    products = jnp.where(leading, rotated(w, 1), rotated(w, 2)) * jnp.where(
        leading, rotated(p, 2), rotated(p, 1)
    )
    crossed = products - jnp.where(leading, rotated(products, 3), rotated(products, 5))
    high, low = parts_of(crossed, 2)
    moments = jnp.concatenate([strengths, jnp.where(leading, high, low)], 0).astype(bf16)
    return features, moments


def target_rows(x):
    high, low = parts_of(x, 2)
    norms = parts_of(norm_sq(high + low) + sigma_sq, 3)
    none = jnp.zeros((2, x.shape[1]), f32)
    one = jnp.ones_like(x)
    high, low = -2.0 * high, -2.0 * low
    rows = [high, high, none, low, low, none, one, one, none, one, *norms, none]
    return jnp.concatenate(rows, 0).astype(bf16)


def field(blocks, x):
    width = x.shape[1]
    center = jnp.mean(x, axis=1, keepdims=True)
    leading = lax.broadcasted_iota(jnp.int32, (rows_cycle, width), 0) < 3
    centers = cyclic(jnp.broadcast_to(center, x.shape))
    x = x - center
    targets = target_rows(x)
    total = jnp.zeros((2 * rows_cycle, width), f32)
    for begin in range(0, len(blocks), part_blocks):
        rows = [
            source_rows(cyclic(p) - centers, cyclic(w), leading)
            for p, w in blocks[begin : begin + part_blocks]
        ]
        features = jnp.concatenate([pair[0] for pair in rows], 1)
        moments = jnp.concatenate([pair[1] for pair in rows], 1)
        sq = lax.dot_general(
            features, targets, (((0,), (0,)), ((), ())), preferred_element_type=f32
        )
        root = lax.rsqrt(sq)
        kernel = (root * root * root).astype(bf16)
        total = total + jnp.dot(moments, kernel, preferred_element_type=f32)
    return cross(total[0:3] + total[3:6], x) - (total[8:11] - total[11:14])


def quad(row, a, b, c):
    return dt_slice * (row[0] * a + row[1] * b + row[2] * c)


lane = 128


def wide(ref, *index):
    return jnp.concatenate([ref[(*index, chunk)] for chunk in range(ref.shape[-2])], 1)


def store_chunks(ref, value):
    for chunk in range(ref.shape[-2]):
        ref[:, chunk] = value[:, chunk * lane : (chunk + 1) * lane]


def spread_out(ref, value):
    for number in range(ref.shape[0]):
        store_chunks(ref.at[number], value)


def prepare_kernel(
    nodes_hbm,
    vorticity_hbm,
    coarse_hbm,
    own_ref,
    mine_ref,
    send_ref,
    nodes_ref,
    vorticity_ref,
    coarse_ref,
    arrived,
):
    pairs = [(nodes_hbm, nodes_ref), (vorticity_hbm, vorticity_ref), (coarse_hbm, coarse_ref)]
    copies = [
        pltpu.make_async_copy(source, target, arrived.at[number])
        for number, (source, target) in enumerate(pairs)
    ]
    for copy in copies:
        copy.start()
    for copy in copies:
        copy.wait()
    own = nodes_ref[:, 0]
    mine = coarse_ref[...].astype(f32)
    own_ref[...] = own
    mine_ref[...] = mine
    spread_out(send_ref, jnp.concatenate([own, vorticity_ref[...], mine], 0))


def nodes_kernel(all_ref, own_ref, velocity_ref, second_ref, send_ref):
    halves, lines = all_ref.shape[:2]
    found = []
    for node in range(3):
        rows = pl.ds(3 * node, 3)
        blocks = [
            (wide(all_ref, h, z, rows), wide(all_ref, h, z, pl.ds(9, 3)))
            for z in range(lines)
            for h in range(halves)
        ]
        found.append(field(blocks, own_ref[rows]))
    velocity_ref[...] = jnp.concatenate(found, 0)
    second = own_ref[0:3] + quad(node_weights[0], *found)
    second_ref[...] = second
    spread_out(send_ref, second)


def swept_blocks(all_ref, gathered_ref):
    halves, lines = all_ref.shape[:2]
    return [
        (wide(gathered_ref, halves * z + h, pl.ds(0, 3)), wide(all_ref, h, z, pl.ds(9, 3)))
        for z in range(lines)
        for h in range(halves)
    ]


def second_kernel(
    all_ref, gathered_ref, velocity_ref, second_ref, swept_ref, third_ref, send_ref
):
    second = second_ref[...]
    blocks = swept_blocks(all_ref, gathered_ref)
    swept = field(blocks, second)
    swept_ref[...] = swept
    nodes = [velocity_ref[pl.ds(3 * node, 3)] for node in range(3)]
    third = second + 0.5 * dt_slice * (swept - nodes[1]) + quad(node_weights[1], *nodes)
    third_ref[...] = third
    spread_out(send_ref, third)


def third_kernel(
    all_ref, gathered_ref, velocity_ref, swept_ref, third_ref, send_ref
):
    third = third_ref[...]
    blocks = swept_blocks(all_ref, gathered_ref)
    last = field(blocks, third)
    early = quad(node_weights[0], velocity_ref[0:3], swept_ref[...], last)
    late = quad(node_weights[1], velocity_ref[0:3], swept_ref[...], last)
    chunks = early.shape[1] // lane
    for number in range(send_ref.shape[0]):
        for chunk in range(chunks):
            lanes = slice(chunk * lane, (chunk + 1) * lane)
            send_ref[number, :, chunk] = early[:, lanes]
            send_ref[number, :, chunks + chunk] = (early + late)[:, lanes]


def means_kernel(all_ref, second_ref, third_ref, quads_ref, mine_ref, means_ref, send_ref):
    halves, lines = all_ref.shape[:2]
    width = mine_ref.shape[1]
    ones = jnp.ones((1, width), f32)
    rows, coarse = [], []
    for z in range(lines):
        for h in range(halves):
            number = halves * z + h
            both = wide(quads_ref, number, pl.ds(0, 3))
            values = jnp.concatenate(
                [
                    wide(all_ref, h, z, pl.ds(0, 3)),
                    wide(second_ref, number, pl.ds(0, 3)),
                    wide(third_ref, number, pl.ds(0, 3)),
                    both[:, :width],
                    both[:, width:],
                    ones,
                ],
                0,
            )
            rows.append(jnp.concatenate(parts_of(values, 2), 0).astype(bf16))
            coarse.append(all_ref[h, z, 12])
    columns = jnp.concatenate(coarse, 0).T
    mine = mine_ref[...]
    total = jnp.zeros((32, width), f32)
    for begin in range(0, len(rows), part_blocks):
        end = begin + part_blocks
        chunks = range(begin * width // lane, end * width // lane)
        same = [
            jnp.where(columns[:, chunk : chunk + 1] == mine, 1.0, 0.0).astype(bf16)
            for chunk in chunks
        ]
        total = total + jnp.dot(
            jnp.concatenate(rows[begin:end], 1),
            jnp.concatenate(same, 0),
            preferred_element_type=f32,
        )
    total = total[0:16] + total[16:32]
    means = total[0:15] / total[15:16]
    means_ref[...] = means
    first_slice = lax.axis_index("tm") == 0
    spread_out(send_ref, means[12:15] + jnp.where(first_slice, means[0:3], 0.0))


def ends_kernel(received_ref, means_ref, own_ref, second_ref, third_ref, fine_ref, end_ref):
    slice_index = lax.axis_index("tm")
    gathered = jnp.zeros(received_ref.shape[1:], f32)
    for number in range(received_ref.shape[0]):
        gathered = gathered + jnp.where(number < slice_index, received_ref[number], 0.0)
    gathered = jnp.concatenate([gathered[:, chunk] for chunk in range(gathered.shape[1])], 1)
    begin = jnp.where(slice_index == 0, means_ref[0:3], gathered)
    finish = begin + means_ref[12:15]
    fine_ref[0:3, 0] = own_ref[0:3] + (begin - means_ref[0:3])
    fine_ref[3:6, 0] = second_ref[...] + ((begin + means_ref[9:12]) - means_ref[3:6])
    fine_ref[6:9, 0] = third_ref[...] + (finish - means_ref[6:9])
    width, half = finish.shape[1], end_ref.shape[2]
    even = lax.broadcasted_iota(jnp.int32, (width, half), 0) == 2 * lax.broadcasted_iota(
        jnp.int32, (width, half), 1
    )
    pick = jnp.where(even, 1.0, 0.0).astype(bf16)
    stacked = jnp.concatenate(parts_of(finish, 3), 0).astype(bf16)
    picked = jnp.dot(stacked, pick, preferred_element_type=f32)
    end_ref[:, 0] = picked[0:3] + picked[3:6] + picked[6:9]


def call(kernel, shapes, *operands):
    return pl.pallas_call(
        kernel,
        out_shape=[jax.ShapeDtypeStruct(shape, f32) for shape in shapes],
        compiler_params=pltpu.CompilerParams(vmem_limit_bytes=vmem_bytes),
    )(*operands)


def prepare(node_pos, vorticity, coarse_of, copies):
    width = vorticity.shape[1]
    nodes = node_pos.reshape(9, 1, width)
    coarse = coarse_of[None]
    shapes = [(9, width), (1, width), (copies, 13, width // lane, lane)]
    return pl.pallas_call(
        prepare_kernel,
        out_shape=[jax.ShapeDtypeStruct(shape, f32) for shape in shapes],
        in_specs=[pl.BlockSpec(memory_space=pltpu.HBM)] * 3,
        scratch_shapes=[
            pltpu.VMEM(nodes.shape, f32),
            pltpu.VMEM(vorticity.shape, f32),
            pltpu.VMEM(coarse.shape, jnp.int32),
            pltpu.SemaphoreType.DMA((3,)),
        ],
        compiler_params=pltpu.CompilerParams(vmem_limit_bytes=vmem_bytes),
    )(*[pltpu.with_memory_space_constraint(x, pltpu.HBM) for x in (nodes, vorticity, coarse)])


def body(node_pos, vorticity, coarse_of):
    width = vorticity.shape[1]
    domains = lax.axis_size("dom")
    slices = lax.axis_size("tm")
    lines = domains // 2
    chunks = width // lane
    same_core = [[2 * z + h for z in range(lines)] for h in range(2)]
    same_chip = [[2 * z, 2 * z + 1] for z in range(lines)]
    own, mine, send = prepare(node_pos, vorticity, coarse_of, lines)
    along = lax.all_to_all(send, "dom", 0, 0, axis_index_groups=same_core)
    everyone = lax.all_gather(along, "dom", axis=0, axis_index_groups=same_chip)
    three = (3, width)
    packed = (3, chunks, lane)
    velocity, second, send = call(
        nodes_kernel, [(9, width), three, (domains,) + packed], everyone, own
    )
    seconds = lax.all_to_all(send, "dom", 0, 0)
    swept, third, send = call(
        second_kernel,
        [three, three, (domains,) + packed],
        everyone,
        seconds,
        velocity,
        second,
    )
    thirds = lax.all_to_all(send, "dom", 0, 0)
    (send,) = call(
        third_kernel,
        [(domains, 3, 2 * chunks, lane)],
        everyone,
        thirds,
        velocity,
        swept,
        third,
    )
    quads = lax.all_to_all(send, "dom", 0, 0)
    means, send = call(
        means_kernel,
        [(15, width), (slices,) + packed],
        everyone,
        seconds,
        thirds,
        quads,
        mine,
    )
    received = lax.all_to_all(send, "tm", 0, 0)
    fine_nodes, coarse_end = call(
        ends_kernel,
        [(9, 1, width), (3, 1, width // 2)],
        received,
        means,
        own,
        second,
        third,
    )
    return fine_nodes.reshape(node_pos.shape), coarse_end.reshape(1, 3, width // 2)


def solution(mesh):
    return jax.shard_map(
        body,
        mesh=mesh,
        in_specs=(P("tm", None, None, "dom"), P(None, "dom"), P("dom")),
        out_specs=(P("tm", None, None, "dom"), P("tm", None, "dom")),
        check_vma=False,
    )
```

```python
import math

import jax
import jax.numpy as jnp
from jax import lax
from jax.experimental import pallas as pl
from jax.experimental.pallas import tpu as pltpu
from jax.sharding import PartitionSpec as P

f32 = jnp.float32
bf16 = jnp.bfloat16
inv_four_pi = 1.0 / (4.0 * math.pi)
sigma_sq = 0.01
dt_slice = 0.5
node_weights = ((5.0 / 24.0, 1.0 / 3.0, -1.0 / 24.0), (-1.0 / 24.0, 1.0 / 3.0, 5.0 / 24.0))
vmem_bytes = 52 << 20
part_blocks = 2
rows_cycle = 8


def high_part(value):
    return value.astype(bf16).astype(f32)


def parts_of(value, number):
    found = []
    for _ in range(number - 1):
        high = high_part(value)
        found.append(high)
        value = value - high
    found.append(high_part(value))
    return found


def norm_sq(rows):
    return rows[0:1] * rows[0:1] + rows[1:2] * rows[1:2] + rows[2:3] * rows[2:3]


def cross(a, b):
    return jnp.concatenate(
        [
            a[1:2] * b[2:3] - a[2:3] * b[1:2],
            a[2:3] * b[0:1] - a[0:1] * b[2:3],
            a[0:1] * b[1:2] - a[1:2] * b[0:1],
        ],
        0,
    )


def cyclic(rows):
    return jnp.concatenate([rows, rows, rows[0:2]], 0)


def rotated(rows, number):
    return pltpu.roll(rows, rows_cycle - number, 0)


def strength_rows(w, leading):
    w = cyclic(w) * inv_four_pi
    high, low = parts_of(w, 2)
    turned = jnp.where(leading, rotated(w, 1), rotated(w, 2))
    return jnp.where(leading, high, low), turned


def source_rows(p, strengths, turned, leading):
    high, low = parts_of(p, 2)
    near = jnp.where(leading, high, low)
    summed = high + low
    first, second, third = parts_of(summed * summed, 3)
    norms = jnp.where(leading, first, second)
    last = jnp.where(leading, third, 1.0)
    features = jnp.concatenate([near, near, norms, last], 0).astype(bf16)
    products = turned * jnp.where(leading, rotated(p, 2), rotated(p, 1))
    crossed = products - jnp.where(leading, rotated(products, 3), rotated(products, 5))
    high, low = parts_of(crossed, 2)
    moments = jnp.concatenate([strengths, jnp.where(leading, high, low)], 0).astype(bf16)
    return features, moments


def target_rows(x):
    high, low = parts_of(x, 2)
    norms = parts_of(norm_sq(high + low) + sigma_sq, 3)
    none = jnp.zeros((2, x.shape[1]), f32)
    one = jnp.ones_like(x)
    high, low = -2.0 * high, -2.0 * low
    rows = [high, high, none, low, low, none, one, one, none, one, *norms, none]
    return jnp.concatenate(rows, 0).astype(bf16)


def field(blocks, x):
    width = x.shape[1]
    center = jnp.mean(x, axis=1, keepdims=True)
    leading = lax.broadcasted_iota(jnp.int32, (rows_cycle, width), 0) < 3
    centers = cyclic(jnp.broadcast_to(center, x.shape))
    x = x - center
    targets = target_rows(x)
    total = jnp.zeros((2 * rows_cycle, width), f32)
    for begin in range(0, len(blocks), part_blocks):
        rows = [
            source_rows(cyclic(p) - centers, *w, leading)
            for p, w in blocks[begin : begin + part_blocks]
        ]
        features = jnp.concatenate([pair[0] for pair in rows], 1)
        moments = jnp.concatenate([pair[1] for pair in rows], 1)
        sq = lax.dot_general(
            features, targets, (((0,), (0,)), ((), ())), preferred_element_type=f32
        )
        root = lax.rsqrt(sq)
        kernel = (root * root * root).astype(bf16)
        total = total + jnp.dot(moments, kernel, preferred_element_type=f32)
    return cross(total[0:3] + total[3:6], x) - (total[8:11] - total[11:14])


def quad(row, a, b, c):
    return dt_slice * (row[0] * a + row[1] * b + row[2] * c)


lane = 128


def wide(ref, *index):
    return jnp.concatenate([ref[(*index, chunk)] for chunk in range(ref.shape[-2])], 1)


def store_chunks(ref, value):
    for chunk in range(ref.shape[-2]):
        ref[:, chunk] = value[:, chunk * lane : (chunk + 1) * lane]


def spread_out(ref, value):
    for number in range(ref.shape[0]):
        store_chunks(ref.at[number], value)


def prepare_kernel(
    nodes_hbm,
    vorticity_hbm,
    coarse_hbm,
    own_ref,
    mine_ref,
    send_ref,
    nodes_ref,
    vorticity_ref,
    coarse_ref,
    arrived,
):
    pairs = [(nodes_hbm, nodes_ref), (vorticity_hbm, vorticity_ref), (coarse_hbm, coarse_ref)]
    copies = [
        pltpu.make_async_copy(source, target, arrived.at[number])
        for number, (source, target) in enumerate(pairs)
    ]
    for copy in copies:
        copy.start()
    for copy in copies:
        copy.wait()
    own = nodes_ref[:, 0]
    mine = coarse_ref[...].astype(f32)
    own_ref[...] = own
    mine_ref[...] = mine
    spread_out(send_ref, jnp.concatenate([own, vorticity_ref[...], mine], 0))


def nodes_kernel(all_ref, own_ref, velocity_ref, second_ref, send_ref, strengths_ref):
    halves, lines = all_ref.shape[:2]
    width = own_ref.shape[1]
    leading = lax.broadcasted_iota(jnp.int32, (rows_cycle, width), 0) < 3
    places = [(h, z) for z in range(lines) for h in range(halves)]
    strengths = [strength_rows(wide(all_ref, h, z, pl.ds(9, 3)), leading) for h, z in places]
    for number, pair in enumerate(strengths):
        strengths_ref[number] = jnp.concatenate(pair, 0)
    found = []
    for node in range(3):
        rows = pl.ds(3 * node, 3)
        blocks = [
            (wide(all_ref, h, z, rows), pair)
            for (h, z), pair in zip(places, strengths, strict=True)
        ]
        found.append(field(blocks, own_ref[rows]))
    velocity_ref[...] = jnp.concatenate(found, 0)
    second = own_ref[0:3] + quad(node_weights[0], *found)
    second_ref[...] = second
    spread_out(send_ref, second)


def swept_blocks(strengths_ref, gathered_ref):
    return [
        (
            wide(gathered_ref, number, pl.ds(0, 3)),
            (strengths_ref[number, 0:rows_cycle], strengths_ref[number, rows_cycle:]),
        )
        for number in range(gathered_ref.shape[0])
    ]


def second_kernel(
    strengths_ref, gathered_ref, velocity_ref, second_ref, swept_ref, third_ref, send_ref
):
    second = second_ref[...]
    blocks = swept_blocks(strengths_ref, gathered_ref)
    swept = field(blocks, second)
    swept_ref[...] = swept
    nodes = [velocity_ref[pl.ds(3 * node, 3)] for node in range(3)]
    third = second + 0.5 * dt_slice * (swept - nodes[1]) + quad(node_weights[1], *nodes)
    third_ref[...] = third
    spread_out(send_ref, third)


def third_kernel(
    strengths_ref, gathered_ref, velocity_ref, swept_ref, third_ref, send_ref
):
    third = third_ref[...]
    blocks = swept_blocks(strengths_ref, gathered_ref)
    last = field(blocks, third)
    early = quad(node_weights[0], velocity_ref[0:3], swept_ref[...], last)
    late = quad(node_weights[1], velocity_ref[0:3], swept_ref[...], last)
    chunks = early.shape[1] // lane
    for number in range(send_ref.shape[0]):
        for chunk in range(chunks):
            lanes = slice(chunk * lane, (chunk + 1) * lane)
            send_ref[number, :, chunk] = early[:, lanes]
            send_ref[number, :, chunks + chunk] = (early + late)[:, lanes]


def means_kernel(all_ref, second_ref, third_ref, quads_ref, mine_ref, means_ref, send_ref):
    halves, lines = all_ref.shape[:2]
    width = mine_ref.shape[1]
    ones = jnp.ones((1, width), f32)
    rows, coarse = [], []
    for z in range(lines):
        for h in range(halves):
            number = halves * z + h
            both = wide(quads_ref, number, pl.ds(0, 3))
            values = jnp.concatenate(
                [
                    wide(all_ref, h, z, pl.ds(0, 3)),
                    wide(second_ref, number, pl.ds(0, 3)),
                    wide(third_ref, number, pl.ds(0, 3)),
                    both[:, :width],
                    both[:, width:],
                    ones,
                ],
                0,
            )
            rows.append(jnp.concatenate(parts_of(values, 2), 0).astype(bf16))
            coarse.append(all_ref[h, z, 12])
    columns = jnp.concatenate(coarse, 0).T
    mine = mine_ref[...]
    total = jnp.zeros((32, width), f32)
    for begin in range(0, len(rows), part_blocks):
        end = begin + part_blocks
        chunks = range(begin * width // lane, end * width // lane)
        same = [
            jnp.where(columns[:, chunk : chunk + 1] == mine, 1.0, 0.0).astype(bf16)
            for chunk in chunks
        ]
        total = total + jnp.dot(
            jnp.concatenate(rows[begin:end], 1),
            jnp.concatenate(same, 0),
            preferred_element_type=f32,
        )
    total = total[0:16] + total[16:32]
    means = total[0:15] / total[15:16]
    means_ref[...] = means
    first_slice = lax.axis_index("tm") == 0
    spread_out(send_ref, means[12:15] + jnp.where(first_slice, means[0:3], 0.0))


def ends_kernel(received_ref, means_ref, own_ref, second_ref, third_ref, fine_ref, end_ref):
    slice_index = lax.axis_index("tm")
    gathered = jnp.zeros(received_ref.shape[1:], f32)
    for number in range(received_ref.shape[0]):
        gathered = gathered + jnp.where(number < slice_index, received_ref[number], 0.0)
    gathered = jnp.concatenate([gathered[:, chunk] for chunk in range(gathered.shape[1])], 1)
    begin = jnp.where(slice_index == 0, means_ref[0:3], gathered)
    finish = begin + means_ref[12:15]
    fine_ref[0:3, 0] = own_ref[0:3] + (begin - means_ref[0:3])
    fine_ref[3:6, 0] = second_ref[...] + ((begin + means_ref[9:12]) - means_ref[3:6])
    fine_ref[6:9, 0] = third_ref[...] + (finish - means_ref[6:9])
    width, half = finish.shape[1], end_ref.shape[2]
    even = lax.broadcasted_iota(jnp.int32, (width, half), 0) == 2 * lax.broadcasted_iota(
        jnp.int32, (width, half), 1
    )
    pick = jnp.where(even, 1.0, 0.0).astype(bf16)
    stacked = jnp.concatenate(parts_of(finish, 3), 0).astype(bf16)
    picked = jnp.dot(stacked, pick, preferred_element_type=f32)
    end_ref[:, 0] = picked[0:3] + picked[3:6] + picked[6:9]


def call(kernel, shapes, *operands):
    return pl.pallas_call(
        kernel,
        out_shape=[jax.ShapeDtypeStruct(shape, f32) for shape in shapes],
        compiler_params=pltpu.CompilerParams(vmem_limit_bytes=vmem_bytes),
    )(*operands)


def prepare(node_pos, vorticity, coarse_of, copies):
    width = vorticity.shape[1]
    nodes = node_pos.reshape(9, 1, width)
    coarse = coarse_of[None]
    shapes = [(9, width), (1, width), (copies, 13, width // lane, lane)]
    return pl.pallas_call(
        prepare_kernel,
        out_shape=[jax.ShapeDtypeStruct(shape, f32) for shape in shapes],
        in_specs=[pl.BlockSpec(memory_space=pltpu.HBM)] * 3,
        scratch_shapes=[
            pltpu.VMEM(nodes.shape, f32),
            pltpu.VMEM(vorticity.shape, f32),
            pltpu.VMEM(coarse.shape, jnp.int32),
            pltpu.SemaphoreType.DMA((3,)),
        ],
        compiler_params=pltpu.CompilerParams(vmem_limit_bytes=vmem_bytes),
    )(*[pltpu.with_memory_space_constraint(x, pltpu.HBM) for x in (nodes, vorticity, coarse)])


def body(node_pos, vorticity, coarse_of):
    width = vorticity.shape[1]
    domains = lax.axis_size("dom")
    slices = lax.axis_size("tm")
    lines = domains // 2
    chunks = width // lane
    same_core = [[2 * z + h for z in range(lines)] for h in range(2)]
    same_chip = [[2 * z, 2 * z + 1] for z in range(lines)]
    own, mine, send = prepare(node_pos, vorticity, coarse_of, lines)
    along = lax.all_to_all(send, "dom", 0, 0, axis_index_groups=same_core)
    everyone = lax.all_gather(along, "dom", axis=0, axis_index_groups=same_chip)
    three = (3, width)
    packed = (3, chunks, lane)
    velocity, second, send, strengths = call(
        nodes_kernel, [(9, width), three, (domains,) + packed, (domains, 2 * rows_cycle, width)], everyone, own
    )
    seconds = lax.all_to_all(send, "dom", 0, 0)
    swept, third, send = call(
        second_kernel,
        [three, three, (domains,) + packed],
        strengths,
        seconds,
        velocity,
        second,
    )
    thirds = lax.all_to_all(send, "dom", 0, 0)
    (send,) = call(
        third_kernel,
        [(domains, 3, 2 * chunks, lane)],
        strengths,
        thirds,
        velocity,
        swept,
        third,
    )
    quads = lax.all_to_all(send, "dom", 0, 0)
    means, send = call(
        means_kernel,
        [(15, width), (slices,) + packed],
        everyone,
        seconds,
        thirds,
        quads,
        mine,
    )
    received = lax.all_to_all(send, "tm", 0, 0)
    fine_nodes, coarse_end = call(
        ends_kernel,
        [(9, 1, width), (3, 1, width // 2)],
        received,
        means,
        own,
        second,
        third,
    )
    return fine_nodes.reshape(node_pos.shape), coarse_end.reshape(1, 3, width // 2)


def solution(mesh):
    return jax.shard_map(
        body,
        mesh=mesh,
        in_specs=(P("tm", None, None, "dom"), P(None, "dom"), P("dom")),
        out_specs=(P("tm", None, None, "dom"), P("tm", None, "dom")),
        check_vma=False,
    )
```
